32 devices in a mesh: layer: 4 (over x, core), feat: 8 (over z, y).
Axes of the slice: x: 2, y: 2, z: 4, core: 2. Of those that a mesh axis runs over, the one named last changes fastest.
Arguments:
- inputs: bfloat16 [4, 512, 2304], P('layer', 'feat'), may hold values from -6 to 6
- targets: bfloat16 [4, 512, 2304], P('layer', 'feat'), may hold values from -64 to 64
- enc_weight: bfloat16 [4, 2304, 8192], P('layer', None, 'feat'), may hold values from -0.125 to 0.125
- enc_bias: float32 [4, 8192], P('layer', 'feat'), may hold values from -3 to 3
- dec_weight: bfloat16 [4, 4, 8192, 2304], P('layer', None, 'feat'), may hold values from -0.0625 to 0.0625
- dec_bias: float32 [4, 2304], P('layer'), may hold values from -3 to 3
Outputs:
- enc_grad: float32 [4, 2304, 8192], P('layer', None, 'feat')
- enc_bias_grad: float32 [4, 8192], P('layer', 'feat')
- dec_grad: float32 [4, 4, 8192, 2304], P('layer', None, 'feat')
- dec_bias_grad: float32 [4, 2304], P('layer')
- mean_square: float32 [], replicated
The draws below stay inside these ranges and needn't reach their ends.
All inputs are finite; a program needn't handle non-finite values.
Results may differ from the reference program's by a relative error of at most 0.0095.
Values may be sent and summed in bfloat16 or wider, within the bound.
A program may use at most 192 MiB of HBM per device.

```python
import jax
import jax.numpy as jnp

D = 2304
F = 8192
MB = 128
LAYERS = 4
TOKENS = 512


def draw_targets(key, part):
    key_base = jax.random.fold_in(key, 11)
    base = jnp.clip(jax.random.normal(key_base, (LAYERS, TOKENS, D), jnp.float32), -5.0, 5.0)
    order = (jnp.arange(LAYERS)[:, None] * TOKENS + jnp.arange(TOKENS)[None, :]).astype(jnp.float32)
    rising = 1.0 + 2.0 * order / (LAYERS * TOKENS - 1.0)
    values = base
    values = jnp.clip(values * rising[:, :, None], -64.0, 64.0)
    return values.astype(jnp.bfloat16)


def steps_of(key, dims, pieces, least, top_value):
    factor_of, own = 1.0, jax.random.fold_in(key, 6)
    for position, parts in pieces:
        draws = jnp.exp(jax.random.uniform(jax.random.fold_in(own, position), (parts,), jnp.float32, least / len(pieces), top_value / len(pieces)))
        factor_of = factor_of * jnp.repeat(draws, dims[position] // parts).reshape([-1 if axis == position else 1 for axis in range(len(dims))])
    return factor_of


def bell_draw(own_key, shape, width, most, cuts=(), kind=jnp.bfloat16):
    values = jax.random.normal(own_key, shape, jnp.float32) * width
    if len(cuts) > 0:
        values = steps_of(own_key, shape, cuts, -0.22, 0.18) * values
    return jnp.clip(values, min=-most, max=most).astype(kind)


def setup_inputs(seed: int = 0) -> dict:
    key_of = jax.random.split(jax.random.key(seed), 7)
    inputs = bell_draw(key_of[0], (LAYERS, TOKENS, D), 1.0, 6.0, ((0, 4), (1, 8)))
    targets = draw_targets(jax.random.fold_in(key_of[6], 71), 0)
    enc_weight = bell_draw(key_of[2], (LAYERS, D, F), D ** -0.5, 0.125, ((0, 4), (2, 8)))
    enc_bias = bell_draw(key_of[3], (LAYERS, F), 0.5, 3.0, ((0, 4), (1, 8)), jnp.float32)
    dec_weight = bell_draw(key_of[4], (LAYERS, LAYERS, F, D), F ** -0.5, 0.0625, ((0, 4), (2, 8)))
    dec_bias = bell_draw(key_of[5], (LAYERS, D), 0.5, 3.0, ((0, 4),), jnp.float32)
    return {"inputs": inputs, "targets": targets, "enc_weight": enc_weight, "enc_bias": enc_bias, "dec_weight": dec_weight, "dec_bias": dec_bias}


def reference(inputs, targets, enc_weight, enc_bias, dec_weight, dec_bias):
    depth = inputs.shape[0]
    tok_count = inputs.shape[1]
    model_width = inputs.shape[2]
    pre_list = []
    act_list = []
    for source in range(depth):
        pre_act = jnp.dot(inputs[source], enc_weight[source], preferred_element_type=jnp.float32) + enc_bias[source]
        pre_list.append(pre_act)
        act_list.append(jnp.maximum(pre_act, 0.0).astype(jnp.bfloat16))
    residual_list = []
    squares = jnp.zeros((), jnp.float32)
    bias_rows = []
    for target in range(depth):
        rebuilt = jnp.zeros((tok_count, model_width), jnp.float32) + dec_bias[target]
        for source in range(target + 1):
            rebuilt = rebuilt + jnp.dot(act_list[source], dec_weight[source, target], preferred_element_type=jnp.float32)
        residual = rebuilt - targets[target].astype(jnp.float32)
        squares = squares + jnp.sum(residual * residual)
        bias_rows.append(jnp.sum(residual, axis=0) / MB)
        residual_list.append(residual.astype(jnp.bfloat16))
    mean_square = squares / (depth * tok_count * model_width)
    dec_bias_grad = jnp.stack(bias_rows)
    dec_rows = []
    enc_rows = []
    enc_bias_rows = []
    for source in range(depth):
        slots = []
        grad_act = jnp.zeros(pre_list[source].shape, jnp.float32)
        for target in range(depth):
            if target >= source:
                slots.append(jnp.dot(act_list[source].T, residual_list[target], preferred_element_type=jnp.float32) / MB)
                grad_act = grad_act + jnp.dot(residual_list[target], dec_weight[source, target].T, preferred_element_type=jnp.float32)
            else:
                slots.append(jnp.zeros((dec_weight.shape[2], model_width), jnp.float32))
        dec_rows.append(jnp.stack(slots))
        grad_act = grad_act / MB
        grad_pre = jnp.where(pre_list[source] > 0, grad_act, 0.0)
        enc_bias_rows.append(jnp.sum(grad_pre, axis=0))
        enc_rows.append(jnp.dot(inputs[source].T, grad_pre.astype(jnp.bfloat16), preferred_element_type=jnp.float32))
    return jnp.stack(enc_rows), jnp.stack(enc_bias_rows), jnp.stack(dec_rows), dec_bias_grad, mean_square
```

```python
import functools

import jax
import jax.numpy as jnp
from jax import lax
from jax.experimental import pallas as pl
from jax.experimental.pallas import tpu as pltpu
from jax.sharding import PartitionSpec as P

MB = 128
MESH = pl.DeviceIdType.MESH
VMEM_BYTES = 60 * 1024 * 1024
ROW_TILE = 16


def bits_of(size):
    return size.bit_length() - 1


def flip(index, bit):
    own = (index // (1 << bit)) % 2
    return index + (1 - 2 * own) * (1 << bit), own


def flip_all(index, mask):
    bit = 0
    while mask >> bit:
        if (mask >> bit) & 1:
            index = flip(index, bit)[0]
        bit += 1
    return index


def enter(partners):
    barrier = pltpu.get_barrier_semaphore()
    for partner in partners:
        pl.semaphore_signal(barrier, inc=1, device_id=partner, device_id_type=MESH)
    pl.semaphore_wait(barrier, len(partners))


def gather_orders(n_bits):
    first = list(range(n_bits - 1, -1, -1))
    if n_bits < 2:
        return [first, first]
    second = first[:-2] + [first[-1], first[-2]]
    return [first, second]


def gather_kernel(n_bits, x_ref, out_ref, buf, local_sem, out_sem, send_sem, recv_sem):
    layer = lax.axis_index("layer")
    feat = lax.axis_index("feat")
    rows, width = x_ref.shape
    half = width // 2
    enter([(layer, flip(feat, b)[0]) for b in range(n_bits)])
    own_rows = pl.ds(pl.multiple_of(feat * rows, rows), rows)
    own = pltpu.make_async_copy(x_ref, buf.at[own_rows], local_sem)
    own.start()
    own.wait()
    orders = gather_orders(n_bits)

    def copy(j, slot, mask, bit):
        block = flip_all(feat, mask)
        at = buf.at[
            pl.ds(pl.multiple_of(block * rows, rows), rows), pl.ds(j * half, half)
        ]
        return pltpu.make_async_remote_copy(
            src_ref=at,
            dst_ref=at,
            send_sem=send_sem.at[j, slot],
            recv_sem=recv_sem.at[j, slot],
            device_id=(layer, flip(feat, bit)[0]),
            device_id_type=MESH,
        )

    all_copies = []
    held = [[0], [0]]
    sent = [{}, {}]
    for step in range(n_bits):
        for i in range(1 << step):
            for j in range(2):
                bit = orders[j][step]
                made = copy(j, (1 << step) - 1 + i, held[j][i], bit)
                made.start()
                all_copies.append(made)
                sent[j][step, i] = made
        for i in range(1 << step):
            for j in range(2):
                sent[j][step, i].wait_recv()
        for j in range(2):
            held[j] = held[j] + [m ^ (1 << orders[j][step]) for m in held[j]]
    for made in all_copies:
        made.wait_send()
    done = pltpu.make_async_copy(buf, out_ref, out_sem)
    done.start()
    done.wait()


def gather_tokens(block, feat_size):
    rows, width = block.shape
    n_bits = bits_of(feat_size)
    return pl.pallas_call(
        functools.partial(gather_kernel, n_bits),
        out_shape=jax.ShapeDtypeStruct((rows * feat_size, width), block.dtype),
        in_specs=[pl.BlockSpec(memory_space=pl.ANY)],
        out_specs=pl.BlockSpec(memory_space=pl.ANY),
        scratch_shapes=[
            pltpu.VMEM((rows * feat_size, width), block.dtype),
            pltpu.SemaphoreType.DMA,
            pltpu.SemaphoreType.DMA,
            pltpu.SemaphoreType.DMA((2, feat_size)),
            pltpu.SemaphoreType.DMA((2, feat_size)),
        ],
        compiler_params=pltpu.CompilerParams(
            collective_id=0, has_side_effects=True, vmem_limit_bytes=VMEM_BYTES
        ),
        name="gather_tokens",
    )(block)


def forward_kernel(depth, tiles, x_ref, w_ref, b_ref, dec_ref, bias_ref, goal_ref, pre_ref, act_ref, part_ref):
    layer = lax.axis_index("layer")
    feat = lax.axis_index("feat")
    step = pl.program_id(0)

    @pl.when(step == 0)
    def _():
        pre = jnp.dot(x_ref[...], w_ref[0], preferred_element_type=jnp.float32) + b_ref[...]
        pre_ref[...] = pre
        act_ref[...] = jnp.maximum(pre, 0.0).astype(jnp.bfloat16)

    target = step // tiles

    @pl.when(target >= layer)
    def _():
        part = jnp.dot(act_ref[...], dec_ref[0, 0], preferred_element_type=jnp.float32)
        part_ref[...] = part.astype(jnp.bfloat16)

    @pl.when(target < layer)
    def _():
        part_ref[...] = jnp.zeros_like(part_ref)

    @pl.when(target == layer)
    def _():
        rows = goal_ref.shape[1]
        mine = pl.ds(pl.multiple_of(feat * rows, rows), rows)
        shift = bias_ref[...] - goal_ref[0].astype(jnp.float32)
        part_ref[mine, :] = (part_ref[mine, :].astype(jnp.float32) + shift).astype(jnp.bfloat16)


def tile_of(width):
    for parts in (3, 2):
        if width % (128 * parts) == 0:
            return width // parts
    return width


def forward(gathered, enc_weight, enc_bias, dec_weight, dec_bias, targets):
    tok_count, width = gathered.shape
    feats = enc_weight.shape[2]
    depth = dec_weight.shape[1]
    tile = tile_of(width)
    tiles = width // tile
    rows = targets.shape[1]
    steps = depth * tiles
    return pl.pallas_call(
        functools.partial(forward_kernel, depth, tiles),
        grid=(steps,),
        out_shape=(
            jax.ShapeDtypeStruct((tok_count, feats), jnp.float32),
            jax.ShapeDtypeStruct((tok_count, feats), jnp.bfloat16),
            jax.ShapeDtypeStruct((depth * tok_count, width), jnp.bfloat16),
        ),
        in_specs=[
            pl.BlockSpec((tok_count, width), lambda i: (0, 0)),
            pl.BlockSpec((1, width, feats), lambda i: (0, 0, 0)),
            pl.BlockSpec((1, feats), lambda i: (0, 0)),
            pl.BlockSpec((1, 1, feats, tile), lambda i: (0, i // tiles, 0, i % tiles)),
            pl.BlockSpec((1, tile), lambda i: (0, i % tiles)),
            pl.BlockSpec((1, rows, tile), lambda i: (0, 0, i % tiles)),
        ],
        out_specs=(
            pl.BlockSpec((tok_count, feats), lambda i: (0, 0)),
            pl.BlockSpec((tok_count, feats), lambda i: (0, 0)),
            pl.BlockSpec((tok_count, tile), lambda i: (i // tiles, i % tiles)),
        ),
        compiler_params=pltpu.CompilerParams(vmem_limit_bytes=VMEM_BYTES),
        name="encode_decode",
    )(gathered, enc_weight, enc_bias, dec_weight, dec_bias, targets)


def exchange_kernel(layer_bits, feat_bits, groups, part_ref, out_ref, acc, first, res, *rest):
    n_steps = layer_bits - 1 + feat_bits
    received = rest[:n_steps]
    send_sem, recv_sem, local_sem, out_sem = rest[n_steps:]
    layer = lax.axis_index("layer")
    feat = lax.axis_index("feat")
    total_rows, width = part_ref.shape
    rows = total_rows // groups
    half = width // 2
    cols = half // 3

    sibling, core = flip(layer, 0)
    dims = []
    for b in range(1, layer_bits):
        there, own = flip(layer, b)
        dims.append(((there, feat), own))
    for b in range(feat_bits):
        there, own = flip(feat, b)
        dims.append(((layer, there), own))
    lead = min(3, n_steps)
    orders = []
    for j in range(3):
        turned = [dims[(j + i) % lead] for i in range(lead)]
        orders.append(turned + dims[lead:])
    sibling = (sibling, feat)
    enter([sibling] + [d[0] for d in dims])

    offsets = []
    for j in range(3):
        at = [0]
        for k in range(n_steps):
            at.append(at[-1] + orders[j][k][1] * (rows >> (k + 1)))
        offsets.append(at)

    def span(g, start, size):
        return pl.ds(pl.multiple_of(g * rows + start, ROW_TILE), size)

    def lanes(side, j):
        return pl.ds(pl.multiple_of(side * half + j * cols, 128), cols)

    def local_lanes(j):
        return pl.ds(j * cols, cols)

    copies = []

    def send(g, j, slot, src, dst, partner):
        made = pltpu.make_async_remote_copy(
            src_ref=src,
            dst_ref=dst,
            send_sem=send_sem.at[g, j, slot],
            recv_sem=recv_sem.at[g, j, slot],
            device_id=partner,
            device_id_type=MESH,
        )
        made.start()
        copies.append(made)
        return made

    pending = {}

    def start_scatter(g, j, k):
        partner, own = orders[j][k]
        size = rows >> (k + 1)
        away = offsets[j][k] + (1 - own) * size
        pending[g, j] = send(
            g, j, 1 + k,
            acc.at[span(g, away, size), local_lanes(j)],
            received[k].at[pl.ds(g * size, size), local_lanes(j)],
            partner,
        )

    def start_gather(g, j, k):
        partner, _ = orders[j][k]
        size = rows >> (k + 1)
        at = res.at[span(g, offsets[j][k + 1], size), lanes(core, j)]
        pending[g, j] = send(g, j, 1 + n_steps + k, at, at, partner)

    def stage(g, j, s):
        if s == 0:
            local[g, j].wait()
            pending[g, j].wait_recv()
            at = (span(g, 0, rows), local_lanes(j))
            acc[at] = acc[at] + first[at]
            start_scatter(g, j, 0)
        elif s <= n_steps:
            k = s - 1
            pending[g, j].wait_recv()
            size = rows >> (k + 1)
            keep = span(g, offsets[j][k + 1], size)
            summed = acc[keep, local_lanes(j)] + received[k][pl.ds(g * size, size), local_lanes(j)]
            if k + 1 < n_steps:
                acc[keep, local_lanes(j)] = summed
                start_scatter(g, j, k + 1)
            else:
                res[keep, lanes(core, j)] = summed
                start_gather(g, j, k)
        elif s <= 2 * n_steps:
            k = 2 * n_steps - s
            pending[g, j].wait_recv()
            if k > 0:
                start_gather(g, j, k - 1)
            else:
                at = res.at[span(g, 0, rows), lanes(core, j)]
                pending[g, j] = send(g, j, 1 + 2 * n_steps, at, at, sibling)
        else:
            pending[g, j].wait_recv()

    local = {}
    for g in range(groups):
        for j in range(3):
            pending[g, j] = send(
                g, j, 0,
                part_ref.at[span(g, 0, rows), lanes(1 - core, j)],
                first.at[span(g, 0, rows), local_lanes(j)],
                sibling,
            )
            made = pltpu.make_async_copy(
                part_ref.at[span(g, 0, rows), lanes(core, j)],
                acc.at[span(g, 0, rows), local_lanes(j)],
                local_sem.at[g, j],
            )
            made.start()
            local[g, j] = made
    n_stages = 2 * n_steps + 2
    outs = []
    for wave in range(groups + n_stages - 1):
        for g in range(groups):
            s = wave - g
            if 0 <= s < n_stages:
                for j in range(3):
                    stage(g, j, s)
                if s == n_stages - 1:
                    made = pltpu.make_async_copy(
                        res.at[span(g, 0, rows)],
                        out_ref.at[span(g, 0, rows)],
                        out_sem.at[g],
                    )
                    made.start()
                    outs.append(made)
    for made in copies:
        made.wait_send()
    for made in outs:
        made.wait()


def exchange(parts, layer_size, feat_size, tok_count):
    total_rows, width = parts.shape
    layer_bits, feat_bits = bits_of(layer_size), bits_of(feat_size)
    n_steps = layer_bits - 1 + feat_bits
    rows = max(tok_count, ROW_TILE << n_steps)
    groups = total_rows // rows
    half = width // 2
    slots = 2 * n_steps + 2
    bf16 = jnp.bfloat16
    return pl.pallas_call(
        functools.partial(exchange_kernel, layer_bits, feat_bits, groups),
        out_shape=jax.ShapeDtypeStruct(parts.shape, bf16),
        in_specs=[pl.BlockSpec(memory_space=pl.ANY)],
        out_specs=pl.BlockSpec(memory_space=pl.ANY),
        scratch_shapes=[
            pltpu.VMEM((total_rows, half), bf16),
            pltpu.VMEM((total_rows, half), bf16),
            pltpu.VMEM((total_rows, width), bf16),
        ]
        + [pltpu.VMEM((total_rows >> (k + 1), half), bf16) for k in range(n_steps)]
        + [
            pltpu.SemaphoreType.DMA((groups, 3, slots)),
            pltpu.SemaphoreType.DMA((groups, 3, slots)),
            pltpu.SemaphoreType.DMA((groups, 3)),
            pltpu.SemaphoreType.DMA((groups,)),
        ],
        compiler_params=pltpu.CompilerParams(
            collective_id=1, has_side_effects=True, vmem_limit_bytes=VMEM_BYTES
        ),
        name="exchange_residual",
    )(parts)


def backward_kernel(
    depth, tiles, res_ref, dec_ref, act_ref, pre_ref, x_ref,
    dec_grad_ref, enc_grad_ref, enc_bias_ref, dec_bias_ref, square_ref,
    turned, grad_act, grad_pre, squares,
):
    layer = lax.axis_index("layer")
    step = pl.program_id(0)
    main = depth * tiles
    target = step // tiles
    scale = 1.0 / MB

    @pl.when(step == 0)
    def _():
        turned[...] = act_ref[...].T
        grad_act[...] = jnp.zeros_like(grad_act)
        squares[...] = jnp.zeros_like(squares)

    @pl.when(step < main)
    def _():
        wide = res_ref[...].astype(jnp.float32)
        squares[...] += jnp.sum((wide * wide).reshape(-1, 8, wide.shape[1]), axis=0)

        @pl.when(target == layer)
        def _():
            dec_bias_ref[0, pl.ds(step % tiles, 1), :] = jnp.sum(wide, axis=0, keepdims=True) * scale

    @pl.when((step < main) & (target >= layer))
    def _():
        dec_grad_ref[0, 0] = (
            jnp.dot(turned[...], res_ref[...], preferred_element_type=jnp.float32) * scale
        )
        grad_act[...] += lax.dot_general(
            res_ref[...], dec_ref[0, 0], (((1,), (1,)), ((), ())),
            preferred_element_type=jnp.float32,
        )

    @pl.when((step < main) & (target < layer))
    def _():
        dec_grad_ref[...] = jnp.zeros_like(dec_grad_ref)

    @pl.when(step == main - 1)
    def _():
        grad = jnp.where(pre_ref[...] > 0, grad_act[...] * scale, 0.0)
        enc_bias_ref[...] = jnp.sum(grad, axis=0, keepdims=True)
        grad_pre[...] = grad.astype(jnp.bfloat16)
        square_ref[...] = jnp.sum(squares[...], keepdims=True)

    @pl.when(step >= main)
    def _():
        enc_grad_ref[0] = lax.dot_general(
            x_ref[...], grad_pre[...], (((0,), (0,)), ((), ())),
            preferred_element_type=jnp.float32,
        )


def backward(res, dec_weight, act, pre, gathered):
    tok_count, width = gathered.shape
    feats = act.shape[1]
    depth = dec_weight.shape[1]
    tile = tile_of(width)
    tiles = width // tile
    main = depth * tiles

    def tile_at(i):
        return jnp.minimum(i, main - 1)

    def late(i):
        return jnp.maximum(i - main, 0)

    return pl.pallas_call(
        functools.partial(backward_kernel, depth, tiles),
        grid=(main + tiles,),
        out_shape=(
            jax.ShapeDtypeStruct((1, depth, feats, width), jnp.float32),
            jax.ShapeDtypeStruct((1, width, feats), jnp.float32),
            jax.ShapeDtypeStruct((1, feats), jnp.float32),
            jax.ShapeDtypeStruct((1, tiles, tile), jnp.float32),
            jax.ShapeDtypeStruct((1, 1), jnp.float32),
        ),
        in_specs=[
            pl.BlockSpec((tok_count, tile), lambda i: (tile_at(i) // tiles, tile_at(i) % tiles)),
            pl.BlockSpec(
                (1, 1, feats, tile), lambda i: (0, tile_at(i) // tiles, 0, tile_at(i) % tiles)
            ),
            pl.BlockSpec((tok_count, feats), lambda i: (0, 0)),
            pl.BlockSpec((tok_count, feats), lambda i: (0, 0)),
            pl.BlockSpec((tok_count, tile), lambda i: (0, late(i))),
        ],
        out_specs=(
            pl.BlockSpec(
                (1, 1, feats, tile), lambda i: (0, tile_at(i) // tiles, 0, tile_at(i) % tiles)
            ),
            pl.BlockSpec((1, tile, feats), lambda i: (0, late(i), 0)),
            pl.BlockSpec((1, feats), lambda i: (0, 0)),
            pl.BlockSpec((1, tiles, tile), lambda i: (0, 0, 0)),
            pl.BlockSpec((1, 1), lambda i: (0, 0)),
        ),
        scratch_shapes=[
            pltpu.VMEM((feats, tok_count), jnp.bfloat16),
            pltpu.VMEM((tok_count, feats), jnp.float32),
            pltpu.VMEM((tok_count, feats), jnp.bfloat16),
            pltpu.VMEM((8, tile), jnp.float32),
        ],
        compiler_params=pltpu.CompilerParams(vmem_limit_bytes=VMEM_BYTES),
        name="backward",
    )(res, dec_weight, act, pre, gathered)


def body(layer_size, feat_size, inputs, targets, enc_weight, enc_bias, dec_weight, dec_bias):
    depth = dec_weight.shape[1]
    gathered = gather_tokens(inputs[0], feat_size)
    tok_count, width = gathered.shape
    pre, act, parts = forward(gathered, enc_weight, enc_bias, dec_weight, dec_bias, targets)
    res = exchange(parts, layer_size, feat_size, tok_count)
    dec_grad, enc_grad, enc_bias_grad, dec_bias_grad, squares = backward(
        res, dec_weight, act, pre, gathered
    )
    mean_square = squares[0, 0] / (depth * tok_count * width)
    return enc_grad, enc_bias_grad, dec_grad, dec_bias_grad.reshape(1, width), mean_square


def solution(mesh):
    placed = (
        P("layer", "feat", None),
        P("layer", "feat", None),
        P("layer", None, "feat"),
        P("layer", "feat"),
        P("layer", None, "feat", None),
        P("layer", None),
    )
    return jax.shard_map(
        functools.partial(body, mesh.shape["layer"], mesh.shape["feat"]),
        mesh=mesh,
        in_specs=placed,
        out_specs=(
            P("layer", None, "feat"),
            P("layer", "feat"),
            P("layer", None, "feat", None),
            P("layer", None),
            P(),
        ),
        check_vma=False,
    )
```

```python
import functools

import jax
import jax.numpy as jnp
from jax import lax
from jax.experimental import pallas as pl
from jax.experimental.pallas import tpu as pltpu
from jax.sharding import PartitionSpec as P

MB = 128
MESH = pl.DeviceIdType.MESH
VMEM_BYTES = 60 * 1024 * 1024
ROW_TILE = 16


def bits_of(size):
    return size.bit_length() - 1


def flip(index, bit):
    own = (index // (1 << bit)) % 2
    return index + (1 - 2 * own) * (1 << bit), own


def flip_all(index, mask):
    bit = 0
    while mask >> bit:
        if (mask >> bit) & 1:
            index = flip(index, bit)[0]
        bit += 1
    return index


def enter(partners):
    barrier = pltpu.get_barrier_semaphore()
    for partner in partners:
        pl.semaphore_signal(barrier, inc=1, device_id=partner, device_id_type=MESH)
    pl.semaphore_wait(barrier, len(partners))


def gather_orders(n_bits, parts):
    first = list(range(n_bits - 1, -1, -1))
    if n_bits < 2:
        return [first] * parts
    second = first[:-2] + [first[-1], first[-2]]
    return [second if j % 3 == 1 else first for j in range(parts)]


def gather_kernel(n_bits, parts, x_ref, out_ref, buf, local_sem, out_sem, send_sem, recv_sem):
    layer = lax.axis_index("layer")
    feat = lax.axis_index("feat")
    rows, width = x_ref.shape
    cols = width // parts
    own = pltpu.make_async_copy(
        x_ref, buf.at[pl.ds(pl.multiple_of(feat * rows, rows), rows)], local_sem
    )
    own.start()
    enter([(layer, flip(feat, b)[0]) for b in range(n_bits)])
    own.wait()
    orders = gather_orders(n_bits, parts)

    def copy(j, slot, mask, bit):
        block = flip_all(feat, mask)
        at = buf.at[
            pl.ds(pl.multiple_of(block * rows, rows), rows), pl.ds(j * cols, cols)
        ]
        made = pltpu.make_async_remote_copy(
            src_ref=at,
            dst_ref=at,
            send_sem=send_sem.at[j, slot],
            recv_sem=recv_sem.at[j, slot],
            device_id=(layer, flip(feat, bit)[0]),
            device_id_type=MESH,
        )
        made.start()
        return made

    copies = []
    held = [[0] for _ in range(parts)]
    arriving = [[] for _ in range(parts)]
    for step in range(n_bits):
        for j in range(parts):
            bit = orders[j][step]
            started = []
            for i, mask in enumerate(held[j]):
                if i >= len(held[j]) - len(arriving[j]):
                    arriving[j][i - len(held[j]) + len(arriving[j])].wait_recv()
                started.append(copy(j, (1 << step) - 1 + i, mask, bit))
            copies += started
            arriving[j] = started
            held[j] = held[j] + [m ^ (1 << bit) for m in held[j]]
    for j in range(parts):
        for made in arriving[j]:
            made.wait_recv()
    done = pltpu.make_async_copy(buf, out_ref, out_sem)
    done.start()
    for made in copies:
        made.wait_send()
    done.wait()


def gather_tokens(block, feat_size):
    rows, width = block.shape
    n_bits = bits_of(feat_size)
    parts = next(p for p in (6, 3, 2, 1) if width % (128 * p) == 0)
    return pl.pallas_call(
        functools.partial(gather_kernel, n_bits, parts),
        out_shape=jax.ShapeDtypeStruct((rows * feat_size, width), block.dtype),
        in_specs=[pl.BlockSpec(memory_space=pl.ANY)],
        out_specs=pl.BlockSpec(memory_space=pl.ANY),
        scratch_shapes=[
            pltpu.VMEM((rows * feat_size, width), block.dtype),
            pltpu.SemaphoreType.DMA,
            pltpu.SemaphoreType.DMA,
            pltpu.SemaphoreType.DMA((parts, feat_size)),
            pltpu.SemaphoreType.DMA((parts, feat_size)),
        ],
        compiler_params=pltpu.CompilerParams(
            collective_id=0, has_side_effects=True, vmem_limit_bytes=VMEM_BYTES
        ),
        name="gather_tokens",
    )(block)


def forward_kernel(depth, tiles, x_ref, w_ref, b_ref, dec_ref, bias_ref, goal_ref, pre_ref, act_ref, part_ref):
    layer = lax.axis_index("layer")
    feat = lax.axis_index("feat")
    step = pl.program_id(0)

    @pl.when(step == 0)
    def _():
        pre = jnp.dot(x_ref[...], w_ref[0], preferred_element_type=jnp.float32) + b_ref[...]
        pre_ref[...] = pre
        act_ref[...] = jnp.maximum(pre, 0.0).astype(jnp.bfloat16)

    target = step // tiles

    @pl.when(target >= layer)
    def _():
        part = jnp.dot(act_ref[...], dec_ref[0, 0], preferred_element_type=jnp.float32)
        part_ref[...] = part.astype(jnp.bfloat16)

    @pl.when(target < layer)
    def _():
        part_ref[...] = jnp.zeros_like(part_ref)

    @pl.when(target == layer)
    def _():
        rows = goal_ref.shape[1]
        mine = pl.ds(pl.multiple_of(feat * rows, rows), rows)
        shift = bias_ref[...] - goal_ref[0].astype(jnp.float32)
        part_ref[mine, :] = (part_ref[mine, :].astype(jnp.float32) + shift).astype(jnp.bfloat16)


def tile_of(width):
    for parts in (3, 2):
        if width % (128 * parts) == 0:
            return width // parts
    return width


def forward(gathered, enc_weight, enc_bias, dec_weight, dec_bias, targets):
    tok_count, width = gathered.shape
    feats = enc_weight.shape[2]
    depth = dec_weight.shape[1]
    tile = tile_of(width)
    tiles = width // tile
    rows = targets.shape[1]
    steps = depth * tiles
    return pl.pallas_call(
        functools.partial(forward_kernel, depth, tiles),
        grid=(steps,),
        out_shape=(
            jax.ShapeDtypeStruct((tok_count, feats), jnp.float32),
            jax.ShapeDtypeStruct((tok_count, feats), jnp.bfloat16),
            jax.ShapeDtypeStruct((depth * tok_count, width), jnp.bfloat16),
        ),
        in_specs=[
            pl.BlockSpec((tok_count, width), lambda i: (0, 0)),
            pl.BlockSpec((1, width, feats), lambda i: (0, 0, 0)),
            pl.BlockSpec((1, feats), lambda i: (0, 0)),
            pl.BlockSpec((1, 1, feats, tile), lambda i: (0, i // tiles, 0, i % tiles)),
            pl.BlockSpec((1, tile), lambda i: (0, i % tiles)),
            pl.BlockSpec((1, rows, tile), lambda i: (0, 0, i % tiles)),
        ],
        out_specs=(
            pl.BlockSpec((tok_count, feats), lambda i: (0, 0)),
            pl.BlockSpec((tok_count, feats), lambda i: (0, 0)),
            pl.BlockSpec((tok_count, tile), lambda i: (i // tiles, i % tiles)),
        ),
        compiler_params=pltpu.CompilerParams(vmem_limit_bytes=VMEM_BYTES),
        name="encode_decode",
    )(gathered, enc_weight, enc_bias, dec_weight, dec_bias, targets)


def exchange_kernel(layer_bits, feat_bits, groups, part_ref, out_ref, acc, first, res, *rest):
    n_steps = layer_bits - 1 + feat_bits
    received = rest[:n_steps]
    send_sem, recv_sem, local_sem, out_sem = rest[n_steps:]
    layer = lax.axis_index("layer")
    feat = lax.axis_index("feat")
    total_rows, width = part_ref.shape
    rows = total_rows // groups
    half = width // 2
    cols = half // 3

    sibling, core = flip(layer, 0)
    dims = []
    for b in range(1, layer_bits):
        there, own = flip(layer, b)
        dims.append(((there, feat), own))
    for b in range(feat_bits):
        there, own = flip(feat, b)
        dims.append(((layer, there), own))
    lead = min(3, n_steps)
    orders = []
    for j in range(3):
        turned = [dims[(j + i) % lead] for i in range(lead)]
        orders.append(turned + dims[lead:])
    sibling = (sibling, feat)
    enter([sibling] + [d[0] for d in dims])

    offsets = []
    for j in range(3):
        at = [0]
        for k in range(n_steps):
            at.append(at[-1] + orders[j][k][1] * (rows >> (k + 1)))
        offsets.append(at)

    def span(g, start, size):
        return pl.ds(pl.multiple_of(g * rows + start, ROW_TILE), size)

    def lanes(side, j):
        return pl.ds(pl.multiple_of(side * half + j * cols, 128), cols)

    def local_lanes(j):
        return pl.ds(j * cols, cols)

    copies = []

    def send(g, j, slot, src, dst, partner):
        made = pltpu.make_async_remote_copy(
            src_ref=src,
            dst_ref=dst,
            send_sem=send_sem.at[g, j, slot],
            recv_sem=recv_sem.at[g, j, slot],
            device_id=partner,
            device_id_type=MESH,
        )
        made.start()
        copies.append(made)
        return made

    pending = {}

    def start_scatter(g, j, k):
        partner, own = orders[j][k]
        size = rows >> (k + 1)
        away = offsets[j][k] + (1 - own) * size
        pending[g, j] = send(
            g, j, 1 + k,
            acc.at[span(g, away, size), local_lanes(j)],
            received[k].at[pl.ds(g * size, size), local_lanes(j)],
            partner,
        )

    def start_gather(g, j, k):
        partner, _ = orders[j][k]
        size = rows >> (k + 1)
        at = res.at[span(g, offsets[j][k + 1], size), lanes(core, j)]
        pending[g, j] = send(g, j, 1 + n_steps + k, at, at, partner)

    def stage(g, j, s):
        if s == 0:
            local[g, j].wait()
            pending[g, j].wait_recv()
            at = (span(g, 0, rows), local_lanes(j))
            acc[at] = acc[at] + first[at]
            start_scatter(g, j, 0)
        elif s <= n_steps:
            k = s - 1
            pending[g, j].wait_recv()
            size = rows >> (k + 1)
            keep = span(g, offsets[j][k + 1], size)
            summed = acc[keep, local_lanes(j)] + received[k][pl.ds(g * size, size), local_lanes(j)]
            if k + 1 < n_steps:
                acc[keep, local_lanes(j)] = summed
                start_scatter(g, j, k + 1)
            else:
                res[keep, lanes(core, j)] = summed
                start_gather(g, j, k)
        elif s <= 2 * n_steps:
            k = 2 * n_steps - s
            pending[g, j].wait_recv()
            if k > 0:
                start_gather(g, j, k - 1)
            else:
                at = res.at[span(g, 0, rows), lanes(core, j)]
                pending[g, j] = send(g, j, 1 + 2 * n_steps, at, at, sibling)
        else:
            pending[g, j].wait_recv()

    local = {}
    for g in range(groups):
        for j in range(3):
            pending[g, j] = send(
                g, j, 0,
                part_ref.at[span(g, 0, rows), lanes(1 - core, j)],
                first.at[span(g, 0, rows), local_lanes(j)],
                sibling,
            )
            made = pltpu.make_async_copy(
                part_ref.at[span(g, 0, rows), lanes(core, j)],
                acc.at[span(g, 0, rows), local_lanes(j)],
                local_sem.at[g, j],
            )
            made.start()
            local[g, j] = made
    n_stages = 2 * n_steps + 2
    outs = []
    for wave in range(groups + n_stages - 1):
        for g in range(groups):
            s = wave - g
            if 0 <= s < n_stages:
                for j in range(3):
                    stage(g, j, s)
                if s == n_stages - 1:
                    made = pltpu.make_async_copy(
                        res.at[span(g, 0, rows)],
                        out_ref.at[span(g, 0, rows)],
                        out_sem.at[g],
                    )
                    made.start()
                    outs.append(made)
    for made in copies:
        made.wait_send()
    for made in outs:
        made.wait()


def exchange(parts, layer_size, feat_size, tok_count):
    total_rows, width = parts.shape
    layer_bits, feat_bits = bits_of(layer_size), bits_of(feat_size)
    n_steps = layer_bits - 1 + feat_bits
    rows = max(tok_count, ROW_TILE << n_steps)
    groups = total_rows // rows
    half = width // 2
    slots = 2 * n_steps + 2
    bf16 = jnp.bfloat16
    return pl.pallas_call(
        functools.partial(exchange_kernel, layer_bits, feat_bits, groups),
        out_shape=jax.ShapeDtypeStruct(parts.shape, bf16),
        in_specs=[pl.BlockSpec(memory_space=pl.ANY)],
        out_specs=pl.BlockSpec(memory_space=pl.ANY),
        scratch_shapes=[
            pltpu.VMEM((total_rows, half), bf16),
            pltpu.VMEM((total_rows, half), bf16),
            pltpu.VMEM((total_rows, width), bf16),
        ]
        + [pltpu.VMEM((total_rows >> (k + 1), half), bf16) for k in range(n_steps)]
        + [
            pltpu.SemaphoreType.DMA((groups, 3, slots)),
            pltpu.SemaphoreType.DMA((groups, 3, slots)),
            pltpu.SemaphoreType.DMA((groups, 3)),
            pltpu.SemaphoreType.DMA((groups,)),
        ],
        compiler_params=pltpu.CompilerParams(
            collective_id=1, has_side_effects=True, vmem_limit_bytes=VMEM_BYTES
        ),
        name="exchange_residual",
    )(parts)


def backward_kernel(
    depth, tiles, res_ref, dec_ref, act_ref, pre_ref, x_ref,
    dec_grad_ref, enc_grad_ref, enc_bias_ref, dec_bias_ref, square_ref,
    turned, grad_act, grad_pre, squares,
):
    layer = lax.axis_index("layer")
    step = pl.program_id(0)
    main = depth * tiles
    target = step // tiles
    scale = 1.0 / MB

    @pl.when(step == 0)
    def _():
        turned[...] = act_ref[...].T
        grad_act[...] = jnp.zeros_like(grad_act)
        squares[...] = jnp.zeros_like(squares)

    @pl.when(step < main)
    def _():
        wide = res_ref[...].astype(jnp.float32)
        squares[...] += jnp.sum((wide * wide).reshape(-1, 8, wide.shape[1]), axis=0)

        @pl.when(target == layer)
        def _():
            dec_bias_ref[0, pl.ds(step % tiles, 1), :] = jnp.sum(wide, axis=0, keepdims=True) * scale

    @pl.when((step < main) & (target >= layer))
    def _():
        dec_grad_ref[0, 0] = (
            jnp.dot(turned[...], res_ref[...], preferred_element_type=jnp.float32) * scale
        )
        grad_act[...] += lax.dot_general(
            res_ref[...], dec_ref[0, 0], (((1,), (1,)), ((), ())),
            preferred_element_type=jnp.float32,
        )

    @pl.when((step < main) & (target < layer))
    def _():
        dec_grad_ref[...] = jnp.zeros_like(dec_grad_ref)

    @pl.when(step == main - 1)
    def _():
        grad = jnp.where(pre_ref[...] > 0, grad_act[...] * scale, 0.0)
        enc_bias_ref[...] = jnp.sum(grad, axis=0, keepdims=True)
        grad_pre[...] = grad.astype(jnp.bfloat16)
        square_ref[...] = jnp.sum(squares[...], keepdims=True)

    @pl.when(step >= main)
    def _():
        enc_grad_ref[0] = lax.dot_general(
            x_ref[...], grad_pre[...], (((0,), (0,)), ((), ())),
            preferred_element_type=jnp.float32,
        )


def backward(res, dec_weight, act, pre, gathered):
    tok_count, width = gathered.shape
    feats = act.shape[1]
    depth = dec_weight.shape[1]
    tile = tile_of(width)
    tiles = width // tile
    main = depth * tiles

    def tile_at(i):
        return jnp.minimum(i, main - 1)

    def late(i):
        return jnp.maximum(i - main, 0)

    return pl.pallas_call(
        functools.partial(backward_kernel, depth, tiles),
        grid=(main + tiles,),
        out_shape=(
            jax.ShapeDtypeStruct((1, depth, feats, width), jnp.float32),
            jax.ShapeDtypeStruct((1, width, feats), jnp.float32),
            jax.ShapeDtypeStruct((1, feats), jnp.float32),
            jax.ShapeDtypeStruct((1, tiles, tile), jnp.float32),
            jax.ShapeDtypeStruct((1, 1), jnp.float32),
        ),
        in_specs=[
            pl.BlockSpec((tok_count, tile), lambda i: (tile_at(i) // tiles, tile_at(i) % tiles)),
            pl.BlockSpec(
                (1, 1, feats, tile), lambda i: (0, tile_at(i) // tiles, 0, tile_at(i) % tiles)
            ),
            pl.BlockSpec((tok_count, feats), lambda i: (0, 0)),
            pl.BlockSpec((tok_count, feats), lambda i: (0, 0)),
            pl.BlockSpec((tok_count, tile), lambda i: (0, late(i))),
        ],
        out_specs=(
            pl.BlockSpec(
                (1, 1, feats, tile), lambda i: (0, tile_at(i) // tiles, 0, tile_at(i) % tiles)
            ),
            pl.BlockSpec((1, tile, feats), lambda i: (0, late(i), 0)),
            pl.BlockSpec((1, feats), lambda i: (0, 0)),
            pl.BlockSpec((1, tiles, tile), lambda i: (0, 0, 0)),
            pl.BlockSpec((1, 1), lambda i: (0, 0)),
        ),
        scratch_shapes=[
            pltpu.VMEM((feats, tok_count), jnp.bfloat16),
            pltpu.VMEM((tok_count, feats), jnp.float32),
            pltpu.VMEM((tok_count, feats), jnp.bfloat16),
            pltpu.VMEM((8, tile), jnp.float32),
        ],
        compiler_params=pltpu.CompilerParams(vmem_limit_bytes=VMEM_BYTES),
        name="backward",
    )(res, dec_weight, act, pre, gathered)


def body(layer_size, feat_size, inputs, targets, enc_weight, enc_bias, dec_weight, dec_bias):
    depth = dec_weight.shape[1]
    gathered = gather_tokens(inputs[0], feat_size)
    tok_count, width = gathered.shape
    pre, act, parts = forward(gathered, enc_weight, enc_bias, dec_weight, dec_bias, targets)
    res = exchange(parts, layer_size, feat_size, tok_count)
    dec_grad, enc_grad, enc_bias_grad, dec_bias_grad, squares = backward(
        res, dec_weight, act, pre, gathered
    )
    mean_square = squares[0, 0] / (depth * tok_count * width)
    return enc_grad, enc_bias_grad, dec_grad, dec_bias_grad.reshape(1, width), mean_square


def solution(mesh):
    placed = (
        P("layer", "feat", None),
        P("layer", "feat", None),
        P("layer", None, "feat"),
        P("layer", "feat"),
        P("layer", None, "feat", None),
        P("layer", None),
    )
    return jax.shard_map(
        functools.partial(body, mesh.shape["layer"], mesh.shape["feat"]),
        mesh=mesh,
        in_specs=placed,
        out_specs=(
            P("layer", None, "feat"),
            P("layer", "feat"),
            P("layer", None, "feat", None),
            P("layer", None),
            P(),
        ),
        check_vma=False,
    )
```

```python
import functools

import jax
import jax.numpy as jnp
from jax import lax
from jax.experimental import pallas as pl
from jax.experimental.pallas import tpu as pltpu
from jax.sharding import PartitionSpec as P

MB = 128
MESH = pl.DeviceIdType.MESH
VMEM_BYTES = 60 * 1024 * 1024
ROW_TILE = 16


def bits_of(size):
    return size.bit_length() - 1


def flip(index, bit):
    own = (index // (1 << bit)) % 2
    return index + (1 - 2 * own) * (1 << bit), own


def flip_all(index, mask):
    bit = 0
    while mask >> bit:
        if (mask >> bit) & 1:
            index = flip(index, bit)[0]
        bit += 1
    return index


def enter(partners):
    barrier = pltpu.get_barrier_semaphore()
    for partner in partners:
        pl.semaphore_signal(barrier, inc=1, device_id=partner, device_id_type=MESH)
    pl.semaphore_wait(barrier, len(partners))


def gather_orders(n_bits, parts):
    first = list(range(n_bits - 1, -1, -1))
    if n_bits < 2:
        return [first] * parts
    second = first[:-2] + [first[-1], first[-2]]
    return [second if j % 3 == 1 else first for j in range(parts)]


def gather_kernel(n_bits, parts, x_ref, out_ref, buf, local_sem, out_sem, send_sem, recv_sem):
    layer = lax.axis_index("layer")
    feat = lax.axis_index("feat")
    rows, width = x_ref.shape
    cols = width // parts
    own = pltpu.make_async_copy(
        x_ref, buf.at[pl.ds(pl.multiple_of(feat * rows, rows), rows)], local_sem
    )
    own.start()
    enter([(layer, flip(feat, b)[0]) for b in range(n_bits)])
    own.wait()
    orders = gather_orders(n_bits, parts)

    def copy(j, slot, mask, bit):
        block = flip_all(feat, mask)
        at = buf.at[
            pl.ds(pl.multiple_of(block * rows, rows), rows), pl.ds(j * cols, cols)
        ]
        made = pltpu.make_async_remote_copy(
            src_ref=at,
            dst_ref=at,
            send_sem=send_sem.at[j, slot],
            recv_sem=recv_sem.at[j, slot],
            device_id=(layer, flip(feat, bit)[0]),
            device_id_type=MESH,
        )
        made.start()
        return made

    copies = []
    held = [[0] for _ in range(parts)]
    arriving = [[] for _ in range(parts)]
    for step in range(n_bits):
        for j in range(parts):
            bit = orders[j][step]
            started = []
            for i, mask in enumerate(held[j]):
                if i >= len(held[j]) - len(arriving[j]):
                    arriving[j][i - len(held[j]) + len(arriving[j])].wait_recv()
                started.append(copy(j, (1 << step) - 1 + i, mask, bit))
            copies += started
            arriving[j] = started
            held[j] = held[j] + [m ^ (1 << bit) for m in held[j]]
    for j in range(parts):
        for made in arriving[j]:
            made.wait_recv()
    done = pltpu.make_async_copy(buf, out_ref, out_sem)
    done.start()
    for made in copies:
        made.wait_send()
    done.wait()


def gather_tokens(block, feat_size):
    rows, width = block.shape
    n_bits = bits_of(feat_size)
    parts = next(p for p in (6, 3, 2, 1) if width % (128 * p) == 0)
    return pl.pallas_call(
        functools.partial(gather_kernel, n_bits, parts),
        out_shape=jax.ShapeDtypeStruct((rows * feat_size, width), block.dtype),
        in_specs=[pl.BlockSpec(memory_space=pl.ANY)],
        out_specs=pl.BlockSpec(memory_space=pl.ANY),
        scratch_shapes=[
            pltpu.VMEM((rows * feat_size, width), block.dtype),
            pltpu.SemaphoreType.DMA,
            pltpu.SemaphoreType.DMA,
            pltpu.SemaphoreType.DMA((parts, feat_size)),
            pltpu.SemaphoreType.DMA((parts, feat_size)),
        ],
        compiler_params=pltpu.CompilerParams(
            collective_id=0, has_side_effects=True, vmem_limit_bytes=VMEM_BYTES
        ),
        name="gather_tokens",
    )(block)


def forward_kernel(depth, tiles, x_ref, w_ref, b_ref, dec_ref, bias_ref, goal_ref, pre_ref, act_ref, part_ref):
    layer = lax.axis_index("layer")
    feat = lax.axis_index("feat")
    step = pl.program_id(0)

    @pl.when(step == 0)
    def _():
        pre = jnp.dot(x_ref[...], w_ref[0], preferred_element_type=jnp.float32) + b_ref[...]
        pre_ref[...] = pre
        act_ref[...] = jnp.maximum(pre, 0.0).astype(jnp.bfloat16)

    target = step // tiles

    @pl.when(target >= layer)
    def _():
        part = jnp.dot(act_ref[...], dec_ref[0, 0], preferred_element_type=jnp.float32)
        part_ref[...] = part.astype(jnp.bfloat16)

    @pl.when(target < layer)
    def _():
        part_ref[...] = jnp.zeros_like(part_ref)

    @pl.when(target == layer)
    def _():
        rows = goal_ref.shape[1]
        mine = pl.ds(pl.multiple_of(feat * rows, rows), rows)
        shift = bias_ref[...] - goal_ref[0].astype(jnp.float32)
        part_ref[mine, :] = (part_ref[mine, :].astype(jnp.float32) + shift).astype(jnp.bfloat16)


def tile_of(width):
    for parts in (3, 2):
        if width % (128 * parts) == 0:
            return width // parts
    return width


def forward(gathered, enc_weight, enc_bias, dec_weight, dec_bias, targets):
    tok_count, width = gathered.shape
    feats = enc_weight.shape[2]
    depth = dec_weight.shape[1]
    tile = tile_of(width)
    tiles = width // tile
    rows = targets.shape[1]
    steps = depth * tiles
    return pl.pallas_call(
        functools.partial(forward_kernel, depth, tiles),
        grid=(steps,),
        out_shape=(
            jax.ShapeDtypeStruct((tok_count, feats), jnp.float32),
            jax.ShapeDtypeStruct((tok_count, feats), jnp.bfloat16),
            jax.ShapeDtypeStruct((depth * tok_count, width), jnp.bfloat16),
        ),
        in_specs=[
            pl.BlockSpec((tok_count, width), lambda i: (0, 0)),
            pl.BlockSpec((1, width, feats), lambda i: (0, 0, 0)),
            pl.BlockSpec((1, feats), lambda i: (0, 0)),
            pl.BlockSpec((1, 1, feats, tile), lambda i: (0, i // tiles, 0, i % tiles)),
            pl.BlockSpec((1, tile), lambda i: (0, i % tiles)),
            pl.BlockSpec((1, rows, tile), lambda i: (0, 0, i % tiles)),
        ],
        out_specs=(
            pl.BlockSpec((tok_count, feats), lambda i: (0, 0)),
            pl.BlockSpec((tok_count, feats), lambda i: (0, 0)),
            pl.BlockSpec((tok_count, tile), lambda i: (i // tiles, i % tiles)),
        ),
        compiler_params=pltpu.CompilerParams(vmem_limit_bytes=VMEM_BYTES),
        name="encode_decode",
    )(gathered, enc_weight, enc_bias, dec_weight, dec_bias, targets)


def exchange_kernel(layer_bits, feat_bits, groups, part_ref, out_ref, acc, first, res, *rest):
    n_steps = layer_bits - 1 + feat_bits
    received = rest[:n_steps]
    send_sem, recv_sem, local_sem, out_sem = rest[n_steps:]
    layer = lax.axis_index("layer")
    feat = lax.axis_index("feat")
    total_rows, width = part_ref.shape
    rows = total_rows // groups
    half = width // 2
    cols = half // 3

    sibling, core = flip(layer, 0)
    dims = []
    for b in range(1, layer_bits):
        there, own = flip(layer, b)
        dims.append(((there, feat), own))
    for b in range(feat_bits):
        there, own = flip(feat, b)
        dims.append(((layer, there), own))
    lead = min(3, n_steps)
    orders = []
    for j in range(3):
        turned = [dims[(j + i) % lead] for i in range(lead)]
        orders.append(turned + dims[lead:])
    sibling = (sibling, feat)
    enter([sibling] + [d[0] for d in dims])

    offsets = []
    for j in range(3):
        at = [0]
        for k in range(n_steps):
            at.append(at[-1] + orders[j][k][1] * (rows >> (k + 1)))
        offsets.append(at)

    def span(g, start, size):
        return pl.ds(pl.multiple_of(g * rows + start, ROW_TILE), size)

    def lanes(side, j):
        return pl.ds(pl.multiple_of(side * half + j * cols, 128), cols)

    def local_lanes(j):
        return pl.ds(j * cols, cols)

    copies = []

    def send(g, j, slot, src, dst, partner):
        made = pltpu.make_async_remote_copy(
            src_ref=src,
            dst_ref=dst,
            send_sem=send_sem.at[g, j, slot],
            recv_sem=recv_sem.at[g, j, slot],
            device_id=partner,
            device_id_type=MESH,
        )
        made.start()
        copies.append(made)
        return made

    pending = {}

    def start_scatter(g, j, k):
        partner, own = orders[j][k]
        size = rows >> (k + 1)
        away = offsets[j][k] + (1 - own) * size
        pending[g, j] = send(
            g, j, 1 + k,
            acc.at[span(g, away, size), local_lanes(j)],
            received[k].at[pl.ds(g * size, size), local_lanes(j)],
            partner,
        )

    def start_gather(g, j, k):
        partner, _ = orders[j][k]
        size = rows >> (k + 1)
        at = res.at[span(g, offsets[j][k + 1], size), lanes(core, j)]
        pending[g, j] = send(g, j, 1 + n_steps + k, at, at, partner)

    def stage(g, j, s):
        if s == 0:
            local[g, j].wait()
            pending[g, j].wait_recv()
            at = (span(g, 0, rows), local_lanes(j))
            acc[at] = acc[at] + first[at]
            start_scatter(g, j, 0)
        elif s <= n_steps:
            k = s - 1
            pending[g, j].wait_recv()
            size = rows >> (k + 1)
            keep = span(g, offsets[j][k + 1], size)
            summed = acc[keep, local_lanes(j)] + received[k][pl.ds(g * size, size), local_lanes(j)]
            if k + 1 < n_steps:
                acc[keep, local_lanes(j)] = summed
                start_scatter(g, j, k + 1)
            else:
                res[keep, lanes(core, j)] = summed
                start_gather(g, j, k)
        elif s <= 2 * n_steps:
            k = 2 * n_steps - s
            pending[g, j].wait_recv()
            if k > 0:
                start_gather(g, j, k - 1)
            else:
                at = res.at[span(g, 0, rows), lanes(core, j)]
                pending[g, j] = send(g, j, 1 + 2 * n_steps, at, at, sibling)
        else:
            pending[g, j].wait_recv()

    local = {}
    for g in range(groups):
        for j in range(3):
            pending[g, j] = send(
                g, j, 0,
                part_ref.at[span(g, 0, rows), lanes(1 - core, j)],
                first.at[span(g, 0, rows), local_lanes(j)],
                sibling,
            )
            made = pltpu.make_async_copy(
                part_ref.at[span(g, 0, rows), lanes(core, j)],
                acc.at[span(g, 0, rows), local_lanes(j)],
                local_sem.at[g, j],
            )
            made.start()
            local[g, j] = made
    n_stages = 2 * n_steps + 2
    outs = []
    for wave in range(groups + n_stages - 1):
        for g in (0, 1) if wave == 0 else (wave + 1,):
            if g < groups:
                for j in range(3):
                    stage(g, j, 0)
        for g in range(groups):
            s = wave - g
            if 1 <= s < n_stages:
                for j in range(3):
                    stage(g, j, s)
                if s == n_stages - 1:
                    made = pltpu.make_async_copy(
                        res.at[span(g, 0, rows)],
                        out_ref.at[span(g, 0, rows)],
                        out_sem.at[g],
                    )
                    made.start()
                    outs.append(made)
    for made in copies:
        made.wait_send()
    for made in outs:
        made.wait()


def exchange(parts, layer_size, feat_size, tok_count):
    total_rows, width = parts.shape
    layer_bits, feat_bits = bits_of(layer_size), bits_of(feat_size)
    n_steps = layer_bits - 1 + feat_bits
    rows = max(tok_count, ROW_TILE << n_steps)
    groups = total_rows // rows
    half = width // 2
    slots = 2 * n_steps + 2
    bf16 = jnp.bfloat16
    return pl.pallas_call(
        functools.partial(exchange_kernel, layer_bits, feat_bits, groups),
        out_shape=jax.ShapeDtypeStruct(parts.shape, bf16),
        in_specs=[pl.BlockSpec(memory_space=pl.ANY)],
        out_specs=pl.BlockSpec(memory_space=pl.ANY),
        scratch_shapes=[
            pltpu.VMEM((total_rows, half), bf16),
            pltpu.VMEM((total_rows, half), bf16),
            pltpu.VMEM((total_rows, width), bf16),
        ]
        + [pltpu.VMEM((total_rows >> (k + 1), half), bf16) for k in range(n_steps)]
        + [
            pltpu.SemaphoreType.DMA((groups, 3, slots)),
            pltpu.SemaphoreType.DMA((groups, 3, slots)),
            pltpu.SemaphoreType.DMA((groups, 3)),
            pltpu.SemaphoreType.DMA((groups,)),
        ],
        compiler_params=pltpu.CompilerParams(
            collective_id=1, has_side_effects=True, vmem_limit_bytes=VMEM_BYTES
        ),
        name="exchange_residual",
    )(parts)


def backward_kernel(
    depth, tiles, res_ref, dec_ref, act_ref, pre_ref, x_ref,
    dec_grad_ref, enc_grad_ref, enc_bias_ref, dec_bias_ref, square_ref,
    turned, grad_act, grad_pre, squares,
):
    layer = lax.axis_index("layer")
    step = pl.program_id(0)
    main = depth * tiles
    target = step // tiles
    scale = 1.0 / MB

    @pl.when(step == 0)
    def _():
        turned[...] = act_ref[...].T
        grad_act[...] = jnp.zeros_like(grad_act)
        squares[...] = jnp.zeros_like(squares)

    @pl.when(step < main)
    def _():
        wide = res_ref[...].astype(jnp.float32)
        squares[...] += jnp.sum((wide * wide).reshape(-1, 8, wide.shape[1]), axis=0)

        @pl.when(target == layer)
        def _():
            dec_bias_ref[0, pl.ds(step % tiles, 1), :] = jnp.sum(wide, axis=0, keepdims=True) * scale

    @pl.when((step < main) & (target >= layer))
    def _():
        dec_grad_ref[0, 0] = (
            jnp.dot(turned[...], res_ref[...], preferred_element_type=jnp.float32) * scale
        )
        grad_act[...] += lax.dot_general(
            res_ref[...], dec_ref[0, 0], (((1,), (1,)), ((), ())),
            preferred_element_type=jnp.float32,
        )

    @pl.when((step < main) & (target < layer))
    def _():
        dec_grad_ref[...] = jnp.zeros_like(dec_grad_ref)

    @pl.when(step == main - 1)
    def _():
        grad = jnp.where(pre_ref[...] > 0, grad_act[...] * scale, 0.0)
        enc_bias_ref[...] = jnp.sum(grad, axis=0, keepdims=True)
        grad_pre[...] = grad.astype(jnp.bfloat16)
        square_ref[...] = jnp.sum(squares[...], keepdims=True)

    @pl.when(step >= main)
    def _():
        enc_grad_ref[0] = lax.dot_general(
            x_ref[...], grad_pre[...], (((0,), (0,)), ((), ())),
            preferred_element_type=jnp.float32,
        )


def backward(res, dec_weight, act, pre, gathered):
    tok_count, width = gathered.shape
    feats = act.shape[1]
    depth = dec_weight.shape[1]
    tile = tile_of(width)
    tiles = width // tile
    main = depth * tiles

    def tile_at(i):
        return jnp.minimum(i, main - 1)

    def late(i):
        return jnp.maximum(i - main, 0)

    return pl.pallas_call(
        functools.partial(backward_kernel, depth, tiles),
        grid=(main + tiles,),
        out_shape=(
            jax.ShapeDtypeStruct((1, depth, feats, width), jnp.float32),
            jax.ShapeDtypeStruct((1, width, feats), jnp.float32),
            jax.ShapeDtypeStruct((1, feats), jnp.float32),
            jax.ShapeDtypeStruct((1, tiles, tile), jnp.float32),
            jax.ShapeDtypeStruct((1, 1), jnp.float32),
        ),
        in_specs=[
            pl.BlockSpec((tok_count, tile), lambda i: (tile_at(i) // tiles, tile_at(i) % tiles)),
            pl.BlockSpec(
                (1, 1, feats, tile), lambda i: (0, tile_at(i) // tiles, 0, tile_at(i) % tiles)
            ),
            pl.BlockSpec((tok_count, feats), lambda i: (0, 0)),
            pl.BlockSpec((tok_count, feats), lambda i: (0, 0)),
            pl.BlockSpec((tok_count, tile), lambda i: (0, late(i))),
        ],
        out_specs=(
            pl.BlockSpec(
                (1, 1, feats, tile), lambda i: (0, tile_at(i) // tiles, 0, tile_at(i) % tiles)
            ),
            pl.BlockSpec((1, tile, feats), lambda i: (0, late(i), 0)),
            pl.BlockSpec((1, feats), lambda i: (0, 0)),
            pl.BlockSpec((1, tiles, tile), lambda i: (0, 0, 0)),
            pl.BlockSpec((1, 1), lambda i: (0, 0)),
        ),
        scratch_shapes=[
            pltpu.VMEM((feats, tok_count), jnp.bfloat16),
            pltpu.VMEM((tok_count, feats), jnp.float32),
            pltpu.VMEM((tok_count, feats), jnp.bfloat16),
            pltpu.VMEM((8, tile), jnp.float32),
        ],
        compiler_params=pltpu.CompilerParams(vmem_limit_bytes=VMEM_BYTES),
        name="backward",
    )(res, dec_weight, act, pre, gathered)


def body(layer_size, feat_size, inputs, targets, enc_weight, enc_bias, dec_weight, dec_bias):
    depth = dec_weight.shape[1]
    gathered = gather_tokens(inputs[0], feat_size)
    tok_count, width = gathered.shape
    pre, act, parts = forward(gathered, enc_weight, enc_bias, dec_weight, dec_bias, targets)
    res = exchange(parts, layer_size, feat_size, tok_count)
    dec_grad, enc_grad, enc_bias_grad, dec_bias_grad, squares = backward(
        res, dec_weight, act, pre, gathered
    )
    mean_square = squares[0, 0] / (depth * tok_count * width)
    return enc_grad, enc_bias_grad, dec_grad, dec_bias_grad.reshape(1, width), mean_square


def solution(mesh):
    placed = (
        P("layer", "feat", None),
        P("layer", "feat", None),
        P("layer", None, "feat"),
        P("layer", "feat"),
        P("layer", None, "feat", None),
        P("layer", None),
    )
    return jax.shard_map(
        functools.partial(body, mesh.shape["layer"], mesh.shape["feat"]),
        mesh=mesh,
        in_specs=placed,
        out_specs=(
            P("layer", None, "feat"),
            P("layer", "feat"),
            P("layer", None, "feat", None),
            P("layer", None),
            P(),
        ),
        check_vma=False,
    )
```
